512 devices in a mesh: tm: 32 (over z, core), ha: 4 (over y), wa: 4 (over x).
Axes of the slice: x: 4, y: 4, z: 16, core: 2. Of those that a mesh axis runs over, the one named last changes fastest.
Arguments:
- latents: bfloat16 [128, 48, 96, 16], P('tm', 'ha', 'wa'), may hold values from -6 to 6
- in_weight: bfloat16 [27, 16, 384], replicated, may hold values from -0.3125 to 0.3125
- in_bias: float32 [384], replicated, may hold values from -3 to 3
- norm_gain: float32 [384], replicated, may hold values from 0.1 to 1.9
- mid_weight: bfloat16 [27, 384, 256], replicated, may hold values from -0.0625 to 0.0625
- mid_bias: float32 [256], replicated, may hold values from -3 to 3
- row_heights: int32 [4], replicated, may hold values from 6 to 12, as said below
- col_widths: int32 [4], replicated, may hold values from 12 to 24, as said below
Outputs:
- features: bfloat16 [128, 48, 96, 256], P('tm', 'ha', 'wa')
The draws below stay inside these ranges and needn't reach their ends.
Inputs may be any that keep to these rules, and one draw needn't show every extreme that they name: `row_heights`: the heights sum to 36; one tile row is exactly 12 rows high. `col_widths`: the widths sum to 72; one tile column is exactly 24 columns wide.
All inputs are finite; a program needn't handle non-finite values.
Results may differ from the reference program's by a relative error of at most 0.0051.
Values may be sent and summed in bfloat16 or wider, within the bound.
No kernel may reach another device: no remote copies, remote signals or barrier semaphores. Data moves between devices by JAX's collectives and lax.ppermute only.
A program may use at most 64 MiB of HBM per device.

```python
import jax
import jax.numpy as jnp
from jax import lax

Z = 16
C = 384
CO = 256
TH = 12
TW = 24
FRAMES = 128
FRAME_H = 36
FRAME_W = 72
N_HA = 4
N_WA = 4


def tile_extents(key, count, most):
    key_share, key_order = jax.random.split(key, 2)
    half = most // 2
    share = jax.random.randint(key_share, (), 0, half + 1).astype(jnp.int32)
    extra = jnp.zeros((count,), jnp.int32).at[0].set(half).at[1].set(share).at[2].set(half - share)
    order = jax.random.permutation(key_order, count)
    return (half + extra[order]).astype(jnp.int32)


def draw_row_heights(key, part):
    key = jax.random.fold_in(key, 11)
    return tile_extents(key, N_HA, TH)


def draw_col_widths(key, part):
    key = jax.random.fold_in(key, 23)
    return tile_extents(key, N_WA, TW)


def steps_of(own_key, shape, pieces, least, largest):
    def one(position, parts):
        heights = jax.random.uniform(jax.random.fold_in(jax.random.fold_in(own_key, 6), position), (parts,), jnp.float32, least / len(pieces), largest / len(pieces))
        return jnp.repeat(jnp.exp(heights), shape[position] // parts).reshape((-1,) + (1,) * (len(shape) - position - 1))

    loudness = one(*pieces[0])
    for cut in pieces[1:]:
        loudness = loudness * one(*cut)
    return loudness


def scatter_about(own_key, dims, width, bound, cuts=(), kind=jnp.bfloat16):
    result = jax.random.normal(own_key, dims, jnp.float32) * width
    if len(cuts) > 0:
        result = steps_of(own_key, dims, cuts, -0.22, 0.18) * result
    return jnp.clip(result, min=-bound, max=bound).astype(kind)


def setup_inputs(seed: int = 0) -> dict:
    arg_keys = jax.random.split(jax.random.key(seed), 9)
    return {
        "latents": scatter_about(arg_keys[0], (FRAMES, N_HA * TH, N_WA * TW, Z), 1.0, 6.0, ((0, 32), (1, 4), (2, 4))),
        "in_weight": scatter_about(arg_keys[1], (27, Z, C), (27 * Z) ** -0.5, 0.3125),
        "in_bias": scatter_about(arg_keys[2], (C,), 0.5, 3.0, (), jnp.float32),
        "norm_gain": jnp.clip(1.0 + 0.18 * jax.random.normal(arg_keys[3], (C,), jnp.float32), 0.1, 1.9),
        "mid_weight": scatter_about(arg_keys[4], (27, C, CO), (27 * C) ** -0.5, 0.0625),
        "mid_bias": scatter_about(arg_keys[5], (CO,), 0.5, 3.0, (), jnp.float32),
        "row_heights": draw_row_heights(jax.random.fold_in(arg_keys[8], 71), 0),
        "col_widths": draw_col_widths(jax.random.fold_in(arg_keys[8], 71), 0),
    }


def frame_sources(sizes, tile, total):
    starts = jnp.cumsum(sizes) - sizes
    cells = jnp.arange(total, dtype=jnp.int32)
    which = lax.optimization_barrier(jnp.sum((cells[:, None] >= starts[None, 1:]).astype(jnp.int32), axis=1)).astype(jnp.int32)
    local = cells - jnp.take(starts, which)
    return (which * tile + local).astype(jnp.int32)

def buffer_sources(sizes, tile, total):
    starts = jnp.cumsum(sizes) - sizes
    cells = jnp.arange(sizes.shape[0] * tile, dtype=jnp.int32)
    which = cells // tile
    local = cells % tile
    valid = local < jnp.take(sizes, which)
    source = jnp.clip(jnp.take(starts, which) + local, 0, total - 1).astype(jnp.int32)
    return (source, valid)

def causal_conv(field, kernel_taps):
    taps, inner, outer = kernel_taps.shape
    kernel = kernel_taps.astype(jnp.float32).reshape(3, 3, 3, inner, outer)
    padded = jnp.pad(field.astype(jnp.float32), ((2, 0), (1, 1), (1, 1), (0, 0)))
    return lax.conv_general_dilated(padded[None], kernel, (1, 1, 1), 'VALID', dimension_numbers=('NDHWC', 'DHWIO', 'NDHWC'), precision=lax.Precision.HIGHEST)[0]

def activate(entry, norm_gain):
    values = entry.astype(jnp.float32)
    meansq = lax.optimization_barrier(jnp.mean(values * values, axis=-1, keepdims=True))
    return jax.nn.silu(values * lax.rsqrt(meansq + 1e-06) * norm_gain).astype(jnp.bfloat16)

def reference(latents, in_weight, in_bias, norm_gain, mid_weight, mid_bias, row_heights, col_widths):
    row_src = frame_sources(row_heights, TH, FRAME_H)
    col_src = frame_sources(col_widths, TW, FRAME_W)
    video = jnp.take(jnp.take(latents, row_src, axis=1), col_src, axis=2)
    entry = (causal_conv(video, in_weight) + in_bias).astype(jnp.bfloat16)
    active = activate(entry, norm_gain)
    mixed = entry[..., :CO].astype(jnp.float32) + causal_conv(active, mid_weight) + mid_bias
    row_back, row_ok = buffer_sources(row_heights, TH, FRAME_H)
    col_back, col_ok = buffer_sources(col_widths, TW, FRAME_W)
    placed = jnp.take(jnp.take(mixed, row_back, axis=1), col_back, axis=2)
    keep = row_ok[:, None] & col_ok[None, :]
    return jnp.where(keep[None, :, :, None], placed, 0.0).astype(jnp.bfloat16)
```

```python
import jax
import jax.numpy as jnp
from jax import lax
from jax.experimental import pallas as pl
from jax.experimental.pallas import tpu as pltpu
from jax.sharding import PartitionSpec as P

F = 4
TH, TW = 12, 24
Z, C, CO = 16, 384, 256
NH, NW = 4, 4
LANES = 128
SPAN = 32
RE = TH + 4
RA = TH + 2
MR = F * TW

VM = pltpu.MemorySpace.VMEM
SM = pltpu.MemorySpace.SMEM


def lanes_of():
    return lax.broadcasted_iota(jnp.int32, (Z, LANES), 1) % SPAN


def pack_kernel(rh_ref, cw_ref, lat_ref, blocks_ref, own_ref, f32_ref):
    i, j = lax.axis_index("ha"), lax.axis_index("wa")
    h, w = rh_ref[i], cw_ref[j]
    lane = lanes_of()
    blocks_ref[...] = jnp.zeros_like(blocks_ref)
    f32_ref[...] = jnp.zeros_like(f32_ref)
    for r in range(TH):
        for f in range(F):
            f32_ref[2 + r, :, f * SPAN + 2 : f * SPAN + 2 + TW] = lat_ref[f, r].astype(jnp.float32)
    right = jnp.zeros((Z, LANES), jnp.float32)
    left = jnp.zeros((Z, LANES), jnp.float32)
    for r in range(TH):
        row = f32_ref[2 + r]
        here = (lane // 2) == r
        right = jnp.where(here, pltpu.roll(row, 2 * r - w + LANES, 1), right)
        left = jnp.where(here, pltpu.roll(row, (2 * r - 2) % LANES, 1), left)
    right = right.astype(jnp.bfloat16)
    left = left.astype(jnp.bfloat16)
    own_ref[...] = f32_ref[...].astype(jnp.bfloat16)
    for di in (-1, 0, 1):
        row_in = (i + di >= 0) & (i + di < NH)
        for dj, tile in ((-1, left), (1, right)):
            @pl.when(row_in & (j + dj >= 0) & (j + dj < NW))
            def _(di=di, dj=dj, tile=tile):
                blocks_ref[(i + di) * NW + j + dj, 0:Z] = tile

    @pl.when(i > 0)
    def _():
        for k in range(2):
            blocks_ref[(i - 1) * NW + j, k * Z : (k + 1) * Z] = f32_ref[2 + k].astype(jnp.bfloat16)

    @pl.when(i < NH - 1)
    def _():
        for k in range(2):
            blocks_ref[(i + 1) * NW + j, k * Z : (k + 1) * Z] = f32_ref[h + k].astype(jnp.bfloat16)


def join_kernel(rh_ref, cw_ref, got_ref, own_ref, ext_ref, f32_ref):
    i, j = lax.axis_index("ha"), lax.axis_index("wa")
    h, w = rh_ref[i], cw_ref[j]
    up, down = jnp.maximum(i - 1, 0), jnp.minimum(i + 1, NH - 1)
    hu = rh_ref[up]
    lane = lanes_of()
    to_left, to_right = lane < 2, (lane >= w + 2) & (lane < w + 4)

    def strip(at, k, ok):
        return jnp.where(ok, got_ref[at, k * Z : (k + 1) * Z].astype(jnp.float32), 0.0)

    def sides(row):
        out = []
        for col, ok in ((jnp.maximum(j - 1, 0), j > 0), (jnp.minimum(j + 1, NW - 1), j < NW - 1)):
            row_ok = ok & (row >= 0) & (row < NH)
            out.append(strip(jnp.clip(row, 0, NH - 1) * NW + col, 0, row_ok))
        return out

    def put(at, base, pair, r):
        row = jnp.where(to_left, pltpu.roll(pair[0], LANES - 2 * r, 1), base)
        row = jnp.where(to_right, pltpu.roll(pair[1], LANES + w + 2 - 2 * r, 1), row)
        f32_ref[at] = row

    mid = sides(i)
    for r in range(TH):
        put(2 + r, own_ref[2 + r].astype(jnp.float32), mid, r)
    above, below = sides(i - 1), sides(i + 1)
    for k in range(2):
        put(k, strip(up * NW + j, k, i > 0), above, hu - 2 + k)
    for k in range(2):
        put(h + 2 + k, strip(down * NW + j, k, i < NH - 1), below, k)
    ext_ref[...] = f32_ref[...].astype(jnp.bfloat16)


def main_kernel(
    rh_ref, cw_ref, prev_ref, own_ref, wi_ref, bi_ref, gain_ref, wm_ref, bm_ref,
    out_ref, sa_ref, sb_ref, lhs_ref, short_ref, acc_ref,
):
    t, i, j = lax.axis_index("tm"), lax.axis_index("ha"), lax.axis_index("wa")
    h, w = rh_ref[i], cw_ref[j]
    lane = lax.broadcasted_iota(jnp.int32, (Z, LANES), 1)

    def taps(field, ref, at):
        for dc in range(3):
            piece = field if dc == 0 else pltpu.roll(field, LANES - dc, 1)
            ref[at + dc * Z : at + (dc + 1) * Z] = piece.astype(jnp.bfloat16)

    for r in range(RE):
        prev, own = prev_ref[r].astype(jnp.float32), own_ref[r].astype(jnp.float32)
        one = jnp.where(lane < 3 * SPAN, pltpu.roll(prev, 3 * SPAN, 1), pltpu.roll(own, 3 * SPAN, 1))
        two = jnp.where(lane < 2 * SPAN, pltpu.roll(prev, 2 * SPAN, 1), pltpu.roll(own, 2 * SPAN, 1))
        for dt, field in enumerate((prev, one, two)):
            taps(field, sa_ref, (r * 9 + dt * 3) * Z)
    for r in range(RE - 1):
        own = own_ref[r].astype(jnp.float32)
        nxt = own_ref[r + 1].astype(jnp.float32)
        for dt in range(3):
            a = own if dt == 0 else pltpu.roll(own, LANES - dt * SPAN, 1)
            b = nxt if dt == 2 else pltpu.roll(nxt, (2 - dt) * SPAN, 1)
            taps(jnp.where(lane < 2 * SPAN, a, b), sb_ref, (r * 9 + dt * 3) * Z)

    bias, gain = bi_ref[...], gain_ref[...]
    pos = lax.broadcasted_iota(jnp.int32, (LANES, 1), 0)
    col = pos % SPAN
    col_ok = ((j > 0) | (col > 0)) & ((j < NW - 1) | (col <= w))
    early = (t > 0) | (pos >= 2 * SPAN)

    def row_ok(r):
        return ((i > 0) | (r > 0)) & ((i < NH - 1) | (r <= h))

    def entry_of(s):
        got = lax.dot_general(
            s, wi_ref[...], (((0,), (0,)), ((), ())), preferred_element_type=jnp.float32
        )
        return (got + bias).astype(jnp.bfloat16).astype(jnp.float32)

    def active_of(entry, ok):
        meansq = jnp.mean(entry * entry, axis=-1, keepdims=True)
        v = entry * jnp.where(ok, lax.rsqrt(meansq + 1e-06), 0.0) * gain
        half = 0.5 * v
        return half + half * jnp.tanh(half)

    def step(q, _):
        r = 2 * q
        ents, acts = [], []
        for k in range(2):
            at = pl.multiple_of((r + k) * 9 * Z, Z)
            e = entry_of(sa_ref[pl.ds(at, 27 * Z), :])
            ents.append(e)
            acts.append(active_of(e, col_ok & early & row_ok(r + k)))
        at = pl.multiple_of(r * 9 * Z, Z)
        e = entry_of(sb_ref[pl.ds(at, 27 * Z), :])
        b = active_of(e, col_ok & ((row_ok(r) & (pos < 2 * SPAN)) | (row_ok(r + 1) & (pos >= 2 * SPAN))))
        for k in range(2):
            frames = [acts[k][f * SPAN : (f + 1) * SPAN] for f in range(4)]
            frames += [b[(2 * k + f) * SPAN : (2 * k + f + 1) * SPAN] for f in range(2)]
            m = pl.multiple_of((r + k) * MR, 16)
            for dc in range(3):
                cut = [a[dc : dc + TW] for a in frames]
                for dt in range(3):
                    lhs_ref[pl.ds(m, MR), (dt * 3 + dc) * C : (dt * 3 + dc + 1) * C] = (
                        jnp.concatenate(cut[dt : dt + 4], axis=0).astype(jnp.bfloat16)
                    )
            ef = [ents[k][(2 + f) * SPAN : (3 + f) * SPAN, :CO] for f in range(2)]
            ef += [e[(2 * k + f) * SPAN : (2 * k + f + 1) * SPAN, :CO] for f in range(2)]
            short_ref[pl.ds(m, MR), :] = jnp.concatenate([a[1 : 1 + TW] for a in ef], axis=0)
        return 0

    lax.fori_loop(0, RA // 2, step, 0)

    for dt in range(3):
        for dr in range(3):
            tap = 9 * dt + 3 * dr
            got = jnp.dot(
                lhs_ref[dr * MR : dr * MR + TH * MR, dt * 3 * C : (dt + 1) * 3 * C],
                wm_ref[tap : tap + 3].reshape(3 * C, CO),
                preferred_element_type=jnp.float32,
            )
            if dt == dr == 0:
                acc_ref[...] = got
            else:
                acc_ref[...] += got

    bias_m = bm_ref[...]
    keep_col = lax.broadcasted_iota(jnp.int32, (TW, 1), 0) < w
    for r in range(TH):
        ok = keep_col & (r < h)
        for f in range(F):
            m = r * MR + f * TW
            val = short_ref[m + MR : m + MR + TW] + acc_ref[m : m + TW] + bias_m
            out_ref[f, r] = jnp.where(ok, val, 0.0).astype(jnp.bfloat16)


def per_device(
    latents, in_weight, in_bias, norm_gain, mid_weight, mid_bias, row_heights, col_widths
):
    flipped = jnp.transpose(latents, (0, 1, 3, 2))
    smem, vmem = pl.BlockSpec(memory_space=SM), pl.BlockSpec(memory_space=VM)
    bf16, f32 = jnp.bfloat16, jnp.float32
    blocks, own = pl.pallas_call(
        pack_kernel,
        out_shape=(
            jax.ShapeDtypeStruct((NH * NW, 2 * Z, LANES), bf16),
            jax.ShapeDtypeStruct((RE, Z, LANES), bf16),
        ),
        in_specs=[smem, smem, vmem],
        out_specs=(vmem, vmem),
        scratch_shapes=[pltpu.VMEM((RE, Z, LANES), f32)],
    )(row_heights, col_widths, flipped)
    got = lax.all_to_all(blocks, ("ha", "wa"), 0, 0, tiled=True)
    ext = pl.pallas_call(
        join_kernel,
        out_shape=jax.ShapeDtypeStruct((RE, Z, LANES), bf16),
        in_specs=[smem, smem, vmem, vmem],
        out_specs=vmem,
        scratch_shapes=[pltpu.VMEM((RE, Z, LANES), f32)],
    )(row_heights, col_widths, got, own)
    groups = lax.axis_size("tm")
    prev = lax.ppermute(ext, "tm", [(g, g + 1) for g in range(groups - 1)])
    wi = in_weight.reshape(3, 3, 3, Z, C).transpose(1, 0, 2, 3, 4).reshape(27 * Z, C)
    return pl.pallas_call(
        main_kernel,
        out_shape=jax.ShapeDtypeStruct((F, TH, TW, CO), bf16),
        in_specs=[smem, smem] + [vmem] * 7,
        out_specs=vmem,
        scratch_shapes=[
            pltpu.VMEM((RE * 9 * Z, LANES), bf16),
            pltpu.VMEM((RE * 9 * Z, LANES), bf16),
            pltpu.VMEM((RA * MR, 9 * C), bf16),
            pltpu.VMEM((RA * MR, CO), f32),
            pltpu.VMEM((TH * MR, CO), f32),
        ],
        compiler_params=pltpu.CompilerParams(vmem_limit_bytes=48 * 1024 * 1024),
    )(
        row_heights, col_widths, prev, ext, wi, in_bias.reshape(1, C), norm_gain.reshape(1, C),
        mid_weight, mid_bias.reshape(1, CO),
    )


def solution(mesh):
    placed = (P("tm", "ha", "wa", None), P(), P(), P(), P(), P(), P(), P())
    return jax.shard_map(
        per_device, mesh=mesh, in_specs=placed, out_specs=P("tm", "ha", "wa", None), check_vma=False
    )
```

```python
import jax
import jax.numpy as jnp
from jax import lax
from jax.experimental import pallas as pl
from jax.experimental.pallas import tpu as pltpu
from jax.sharding import PartitionSpec as P

F = 4
TH, TW = 12, 24
Z, C, CO = 16, 384, 256
NH, NW = 4, 4
LANES = 128
SPAN = 32
RE = TH + 4
RA = TH + 2
MR = F * TW
HALF = TH // 2
PR = 2 * TW

VM = pltpu.MemorySpace.VMEM
HBM = pltpu.MemorySpace.HBM


def lanes_of():
    return lax.broadcasted_iota(jnp.int32, (Z, LANES), 1) % SPAN


def name(pairs, sems):
    return [pltpu.make_async_copy(src, dst, sems.at[k]) for k, (src, dst) in enumerate(pairs)]


def fetch(pairs, sems):
    copies = name(pairs, sems)
    for copy in copies:
        copy.start()
    return copies


def pack_kernel(
    rh_hbm, cw_hbm, lat_hbm, blocks_ref, own_ref, f32_ref, lat_ref, rh_ref, cw_ref, sems
):
    copies = fetch(((rh_hbm, rh_ref), (cw_hbm, cw_ref), (lat_hbm, lat_ref)), sems)
    i, j = lax.axis_index("ha"), lax.axis_index("wa")
    lane = lanes_of()
    blocks_ref[...] = jnp.zeros_like(blocks_ref)
    f32_ref[...] = jnp.zeros_like(f32_ref)
    for copy in copies:
        copy.wait()
    h, w = rh_ref[i], cw_ref[j]
    for r in range(TH):
        for f in range(F):
            f32_ref[2 + r, :, f * SPAN + 2 : f * SPAN + 2 + TW] = lat_ref[f, r].astype(jnp.float32)
    right = jnp.zeros((Z, LANES), jnp.float32)
    left = jnp.zeros((Z, LANES), jnp.float32)
    for r in range(TH):
        row = f32_ref[2 + r]
        here = (lane // 2) == r
        right = jnp.where(here, pltpu.roll(row, (2 * r - w + LANES) % LANES, 1), right)
        left = jnp.where(here, pltpu.roll(row, (2 * r - 2) % LANES, 1), left)
    right = right.astype(jnp.bfloat16)
    left = left.astype(jnp.bfloat16)
    own_ref[...] = f32_ref[...].astype(jnp.bfloat16)
    for di in (-1, 0, 1):
        row_in = (i + di >= 0) & (i + di < NH)
        for dj, tile in ((-1, left), (1, right)):
            @pl.when(row_in & (j + dj >= 0) & (j + dj < NW))
            def _(di=di, dj=dj, tile=tile):
                blocks_ref[(i + di) * NW + j + dj, 0:Z] = tile

    @pl.when(i > 0)
    def _():
        for k in range(2):
            blocks_ref[(i - 1) * NW + j, k * Z : (k + 1) * Z] = f32_ref[2 + k].astype(jnp.bfloat16)

    @pl.when(i < NH - 1)
    def _():
        for k in range(2):
            blocks_ref[(i + 1) * NW + j, k * Z : (k + 1) * Z] = f32_ref[h + k].astype(jnp.bfloat16)


def name_weights(sources, outs, scratch):
    wm_hbm, wi_hbm, bi_hbm, gain_hbm, bm_hbm = sources
    u_ref, wi_ref, bi_ref, gain_ref, bm_ref = outs
    mid_ref, wi_raw, sems = scratch
    small = name(
        ((wi_hbm, wi_raw), (bi_hbm, bi_ref), (gain_hbm, gain_ref), (bm_hbm, bm_ref)), sems
    )
    copies = []
    for g in range(3):
        part = pl.ds(g * 3, 3)
        homes = (u_ref.at[0, part], mid_ref.at[part], u_ref.at[3, part])
        copies += name(
            [(wm_hbm.at[pl.ds(9 * dt + 3 * g, 3)], homes[dt]) for dt in range(3)],
            sems.at[pl.ds(4 + 3 * g, 3)],
        )
    return small, copies


def start_weights(sources, outs, scratch):
    small, copies = name_weights(sources, outs, scratch)
    for copy in small + copies:
        copy.start()
    return small, copies


def finish_weights(small, copies, outs, scratch):
    u_ref, wi_ref, bi_ref, gain_ref, bm_ref = outs
    mid_ref, wi_raw, sems = scratch
    for copy in small:
        copy.wait()
    for dr in range(3):
        for dt in range(3):
            for dc in range(3):
                k = dt * 3 + dc
                at = (dr * 8 + k if k < 8 else 24 + dr) * Z
                wi_ref[at : at + Z] = wi_raw[9 * dt + 3 * dr + dc]
    for g in range(3):
        for copy in copies[3 * g : 3 * g + 3]:
            copy.wait()
        for tap in range(3 * g, 3 * g + 3):
            ends = 0.5 * (u_ref[0, tap].astype(jnp.float32) + u_ref[3, tap].astype(jnp.float32))
            mid = 0.5 * mid_ref[tap].astype(jnp.float32)
            u_ref[1, tap] = (ends + mid).astype(jnp.bfloat16)
            u_ref[2, tap] = (ends - mid).astype(jnp.bfloat16)


def join_kernel(*refs):
    rh_hbm, cw_hbm, got_ref, own_ref = refs[:4]
    sources, (ext_ref, size_ref), outs = refs[4:9], refs[9:11], refs[11:16]
    f32_ref, rh_ref, cw_ref, sems = refs[16:20]
    scratch = refs[20:]
    odd = lax.axis_index("tm") % 2 == 1

    @pl.when(odd)
    def _():
        start_weights(sources, outs, scratch)

    copies = fetch(((rh_hbm, rh_ref), (cw_hbm, cw_ref)), sems)
    i, j = lax.axis_index("ha"), lax.axis_index("wa")
    for copy in copies:
        copy.wait()
    h, w = rh_ref[i], cw_ref[j]
    up, down = jnp.maximum(i - 1, 0), jnp.minimum(i + 1, NH - 1)
    hu = rh_ref[up]
    lane = lanes_of()
    to_left, to_right = lane < 2, (lane >= w + 2) & (lane < w + 4)

    def strip(at, k, ok):
        return jnp.where(ok, got_ref[at, k * Z : (k + 1) * Z].astype(jnp.float32), 0.0)

    def sides(row):
        out = []
        for col, ok in ((jnp.maximum(j - 1, 0), j > 0), (jnp.minimum(j + 1, NW - 1), j < NW - 1)):
            row_ok = ok & (row >= 0) & (row < NH)
            out.append(strip(jnp.clip(row, 0, NH - 1) * NW + col, 0, row_ok))
        return out

    def put(at, base, pair, r):
        row = jnp.where(to_left, pltpu.roll(pair[0], (LANES - 2 * r) % LANES, 1), base)
        row = jnp.where(to_right, pltpu.roll(pair[1], (LANES + w + 2 - 2 * r) % LANES, 1), row)
        f32_ref[at] = row

    mid = sides(i)
    for r in range(TH):
        put(2 + r, own_ref[2 + r].astype(jnp.float32), mid, r)
    above, below = sides(i - 1), sides(i + 1)
    for k in range(2):
        put(k, strip(up * NW + j, k, i > 0), above, hu - 2 + k)
    for k in range(2):
        put(h + 2 + k, strip(down * NW + j, k, i < NH - 1), below, k)
    ext_ref[...] = f32_ref[...].astype(jnp.bfloat16)
    size_ref[0:8] = jnp.full((8, LANES), h, jnp.int32)
    size_ref[8:16] = jnp.full((8, LANES), w, jnp.int32)

    @pl.when(odd)
    def _():
        finish_weights(*name_weights(sources, outs, scratch), outs, scratch)


def weight_kernel(*refs):
    sources, outs, scratch = refs[:5], refs[10:15], refs[15:]

    @pl.when(lax.axis_index("tm") % 2 == 0)
    def _():
        finish_weights(*start_weights(sources, outs, scratch), outs, scratch)


def main_kernel(
    prev_ref, own_ref, size_ref, wi_ref, bi_ref, gain_ref, u_ref, bm_ref,
    out_ref, ta_ref, tb_ref, sa_ref, sb_ref, lhs_ref, short_ref, acc_ref,
):
    t, i, j = lax.axis_index("tm"), lax.axis_index("ha"), lax.axis_index("wa")
    h, w = size_ref[0:1, 0:1], size_ref[8:9, 0:1]
    lane = lax.broadcasted_iota(jnp.int32, (Z, LANES), 1)

    def taps(fields, r, turned, last):
        parts = []
        for field in fields:
            for dc in range(3):
                piece = field if dc == 0 else pltpu.roll(field, LANES - dc, 1)
                parts.append(piece.astype(jnp.bfloat16))
        turned[r] = jnp.concatenate(parts[:8], axis=0).T
        last[r * Z : (r + 1) * Z] = parts[8]

    for r in range(RE):
        prev, own = prev_ref[r].astype(jnp.float32), own_ref[r].astype(jnp.float32)
        one = jnp.where(lane < 3 * SPAN, pltpu.roll(prev, 3 * SPAN, 1), pltpu.roll(own, 3 * SPAN, 1))
        two = jnp.where(lane < 2 * SPAN, pltpu.roll(prev, 2 * SPAN, 1), pltpu.roll(own, 2 * SPAN, 1))
        taps((prev, one, two), r, ta_ref, sa_ref)
    for r in range(RE - 1):
        own = own_ref[r].astype(jnp.float32)
        nxt = own_ref[r + 1].astype(jnp.float32)
        fields = []
        for dt in range(3):
            a = own if dt == 0 else pltpu.roll(own, LANES - dt * SPAN, 1)
            b = nxt if dt == 2 else pltpu.roll(nxt, (2 - dt) * SPAN, 1)
            fields.append(jnp.where(lane < 2 * SPAN, a, b))
        taps(fields, r, tb_ref, sb_ref)

    bias, gain = bi_ref[...].reshape(1, C), gain_ref[...].reshape(1, C)
    pos = lax.broadcasted_iota(jnp.int32, (LANES, 1), 0)
    col = pos % SPAN
    col_ok = ((j > 0) | (col > 0)) & ((j < NW - 1) | (col <= w))
    early = (t > 0) | (pos >= 2 * SPAN)

    def row_ok(r):
        return ((i > 0) | (r > 0)) & ((i < NH - 1) | (r <= h))

    def entry_of(r):
        lhs = []
        for at, turned, last in ((r, ta_ref, sa_ref), (r + 1, ta_ref, sa_ref), (r, tb_ref, sb_ref)):
            rest = last[at * Z : (at + 3) * Z].T
            lhs.append(jnp.concatenate([turned[at], turned[at + 1], turned[at + 2], rest], axis=1))
        got = jnp.dot(jnp.concatenate(lhs, axis=0), wi_ref[...], preferred_element_type=jnp.float32)
        return (got + bias).astype(jnp.bfloat16).astype(jnp.float32)

    def active_of(entry, ok):
        meansq = jnp.mean(entry * entry, axis=-1, keepdims=True)
        v = entry * jnp.where(ok, lax.rsqrt(meansq + 1e-06), 0.0) * gain
        half = 0.5 * v
        return half + half * jnp.tanh(half)

    def step(q, _):
        r = 2 * q
        entry = entry_of(r)
        ok = jnp.concatenate(
            [
                col_ok & early & row_ok(r),
                col_ok & early & row_ok(r + 1),
                col_ok & ((row_ok(r) & (pos < 2 * SPAN)) | (row_ok(r + 1) & (pos >= 2 * SPAN))),
            ],
            axis=0,
        )
        active = active_of(entry, ok)
        ents = [entry[k * LANES : (k + 1) * LANES] for k in range(3)]
        acts = [active[k * LANES : (k + 1) * LANES] for k in range(3)]
        e, b = ents[2], acts[2]
        for k in range(2):
            frames = [acts[k][f * SPAN : (f + 1) * SPAN] for f in range(4)]
            frames += [b[(2 * k + f) * SPAN : (2 * k + f + 1) * SPAN] for f in range(2)]
            m = pl.multiple_of((r + k) * PR, 16)
            for p in range(4):
                pair = []
                for a in (frames[:4], frames[2:]):
                    pair.append((a[0] - a[2], a[1] + a[2], a[2] - a[1], a[1] - a[3])[p])
                for dc in range(3):
                    lhs_ref[p, pl.ds(m, PR), dc * C : (dc + 1) * C] = jnp.concatenate(
                        [v[dc : dc + TW] for v in pair], axis=0
                    ).astype(jnp.bfloat16)
            m = pl.multiple_of((r + k) * MR, 16)
            ef = [ents[k][(2 + f) * SPAN : (3 + f) * SPAN, :CO] for f in range(2)]
            ef += [e[(2 * k + f) * SPAN : (2 * k + f + 1) * SPAN, :CO] for f in range(2)]
            short_ref[pl.ds(m, MR), :] = jnp.concatenate([a[1 : 1 + TW] for a in ef], axis=0)
        return 0

    def mid(p, half):
        at = half * HALF * PR
        rows = jnp.concatenate(
            [lhs_ref[p, at + dr * PR : at + (dr + HALF) * PR] for dr in range(3)], axis=1
        )
        acc_ref[p, at : at + HALF * PR] = jnp.dot(
            rows, u_ref[p].reshape(9 * C, CO), preferred_element_type=jnp.float32
        )

    for q in range(HALF // 2 + 1):
        step(q, 0)
    for p in range(4):
        mid(p, 0)
        if HALF // 2 + 1 + p < RA // 2:
            step(HALF // 2 + 1 + p, 0)
    for p in range(4):
        mid(p, 1)

    bias_m = bm_ref[...].reshape(1, CO)
    keep_col = lax.broadcasted_iota(jnp.int32, (TW, 1), 0) < w
    for r in range(TH):
        ok = keep_col & (r < h)
        for pair in range(2):
            m = r * PR + pair * TW
            m0, m1, m2, m3 = (acc_ref[p, m : m + TW] for p in range(4))
            for f, mixed in ((2 * pair, m0 + m1 + m2), (2 * pair + 1, m1 - m2 - m3)):
                at = (r + 1) * MR + f * TW
                val = short_ref[at : at + TW] + mixed + bias_m
                out_ref[f, r] = jnp.where(ok, val, 0.0).astype(jnp.bfloat16)


def per_device(
    latents, in_weight, in_bias, norm_gain, mid_weight, mid_bias, row_heights, col_widths
):
    flipped = jnp.transpose(latents, (0, 1, 3, 2))
    vmem = pl.BlockSpec(memory_space=VM)
    hbm = pl.BlockSpec(memory_space=HBM)

    def stay(*arrays):
        return [pltpu.with_memory_space_constraint(a, HBM) for a in arrays]

    sizes_smem = [pltpu.SMEM((NH,), jnp.int32), pltpu.SMEM((NW,), jnp.int32)]
    bf16, f32 = jnp.bfloat16, jnp.float32
    limit = pltpu.CompilerParams(vmem_limit_bytes=4 * 1024 * 1024)
    blocks, own = pl.pallas_call(
        pack_kernel,
        out_shape=(VM((NH * NW, 2 * Z, LANES), bf16), VM((RE, Z, LANES), bf16)),
        in_specs=[hbm] * 3,
        out_specs=(vmem, vmem),
        scratch_shapes=[
            pltpu.VMEM((RE, Z, LANES), f32),
            pltpu.VMEM((F, TH, Z, TW), bf16),
            *sizes_smem,
            pltpu.SemaphoreType.DMA((3,)),
        ],
        compiler_params=limit,
    )(*stay(row_heights, col_widths, flipped))
    got = lax.all_to_all(blocks, ("ha", "wa"), 0, 0, tiled=True)
    params = stay(mid_weight, in_weight, in_bias, norm_gain, mid_bias)
    ready = (
        VM((4, 9, C, CO), bf16), VM((27 * Z, C), bf16), VM((C,), f32), VM((C,), f32), VM((CO,), f32)
    )
    rooms = [
        pltpu.VMEM((9, C, CO), bf16), pltpu.VMEM((27, Z, C), bf16), pltpu.SemaphoreType.DMA((13,))
    ]
    limit = pltpu.CompilerParams(vmem_limit_bytes=16 * 1024 * 1024)
    ext, sizes, *weights = pl.pallas_call(
        join_kernel,
        out_shape=(VM((RE, Z, LANES), bf16), VM((16, LANES), jnp.int32), *ready),
        in_specs=[hbm, hbm, vmem, vmem] + [hbm] * 5,
        out_specs=(vmem,) * 7,
        scratch_shapes=[
            pltpu.VMEM((RE, Z, LANES), f32), *sizes_smem, pltpu.SemaphoreType.DMA((2,)), *rooms
        ],
        compiler_params=limit,
    )(*stay(row_heights, col_widths), got, own, *params)
    groups = lax.axis_size("tm")
    prev = lax.ppermute(ext, "tm", [(g, g + 1) for g in range(groups - 1)])
    u, wi, bias, gain, bias_m = pl.pallas_call(
        weight_kernel,
        out_shape=ready,
        in_specs=[hbm] * 5 + [vmem] * 5,
        out_specs=(vmem,) * 5,
        scratch_shapes=rooms,
        input_output_aliases={5 + k: k for k in range(5)},
        compiler_params=limit,
        cost_estimate=pl.CostEstimate(flops=10_000_000, bytes_accessed=8_000_000, transcendentals=0),
    )(*params, *weights)
    return pl.pallas_call(
        main_kernel,
        out_shape=jax.ShapeDtypeStruct((F, TH, TW, CO), bf16),
        in_specs=[vmem] * 8,
        out_specs=vmem,
        scratch_shapes=[
            pltpu.VMEM((RE, LANES, LANES), bf16),
            pltpu.VMEM((RE, LANES, LANES), bf16),
            pltpu.VMEM((RE * Z, LANES), bf16),
            pltpu.VMEM((RE * Z, LANES), bf16),
            pltpu.VMEM((4, RA * PR, 3 * C), bf16),
            pltpu.VMEM((RA * MR, CO), f32),
            pltpu.VMEM((4, TH * PR, CO), f32),
        ],
        compiler_params=pltpu.CompilerParams(vmem_limit_bytes=32 * 1024 * 1024),
        cost_estimate=pl.CostEstimate(flops=4_500_000_000, bytes_accessed=8_000_000, transcendentals=1_000_000),
    )(prev, ext, sizes, wi, bias, gain, u, bias_m)


def solution(mesh):
    placed = (P("tm", "ha", "wa", None), P(), P(), P(), P(), P(), P(), P())
    return jax.shard_map(
        per_device, mesh=mesh, in_specs=placed, out_specs=P("tm", "ha", "wa", None), check_vma=False
    )
```

```python
import jax
import jax.numpy as jnp
from jax import lax
from jax.experimental import pallas as pl
from jax.experimental.pallas import tpu as pltpu
from jax.sharding import PartitionSpec as P

F = 4
TH, TW = 12, 24
Z, C, CO = 16, 384, 256
NH, NW = 4, 4
LANES = 128
SPAN = 32
RE = TH + 4
RA = TH + 2
MR = F * TW
HALF = TH // 2
PR = 2 * TW

VM = pltpu.MemorySpace.VMEM
HBM = pltpu.MemorySpace.HBM


def lanes_of():
    return lax.broadcasted_iota(jnp.int32, (Z, LANES), 1) % SPAN


def name(pairs, sems):
    return [pltpu.make_async_copy(src, dst, sems.at[k]) for k, (src, dst) in enumerate(pairs)]


def fetch(pairs, sems):
    copies = name(pairs, sems)
    for copy in copies:
        copy.start()
    return copies


def pack_kernel(
    rh_hbm, cw_hbm, lat_hbm, blocks_ref, own_ref, size_ref, f32_ref, lat_ref, rh_ref, cw_ref, sems
):
    copies = fetch(((rh_hbm, rh_ref), (cw_hbm, cw_ref), (lat_hbm, lat_ref)), sems)
    i, j = lax.axis_index("ha"), lax.axis_index("wa")
    lane = lanes_of()
    blocks_ref[...] = jnp.zeros_like(blocks_ref)
    f32_ref[...] = jnp.zeros_like(f32_ref)
    for copy in copies:
        copy.wait()
    h, w = rh_ref[i], cw_ref[j]
    for k, size in enumerate((h, w, rh_ref[jnp.maximum(i - 1, 0)])):
        size_ref[8 * k : 8 * k + 8] = jnp.full((8, LANES), size, jnp.int32)
    for r in range(TH):
        for f in range(F):
            f32_ref[2 + r, :, f * SPAN + 2 : f * SPAN + 2 + TW] = lat_ref[f, r].astype(jnp.float32)
    right = jnp.zeros((Z, LANES), jnp.float32)
    left = jnp.zeros((Z, LANES), jnp.float32)
    for r in range(TH):
        row = f32_ref[2 + r]
        here = (lane // 2) == r
        right = jnp.where(here, pltpu.roll(row, (2 * r - w + LANES) % LANES, 1), right)
        left = jnp.where(here, pltpu.roll(row, (2 * r - 2) % LANES, 1), left)
    right = right.astype(jnp.bfloat16)
    left = left.astype(jnp.bfloat16)
    own_ref[...] = f32_ref[...].astype(jnp.bfloat16)
    for di in (-1, 0, 1):
        row_in = (i + di >= 0) & (i + di < NH)
        for dj, tile in ((-1, left), (1, right)):
            @pl.when(row_in & (j + dj >= 0) & (j + dj < NW))
            def _(di=di, dj=dj, tile=tile):
                blocks_ref[(i + di) * NW + j + dj, 0:Z] = tile

    @pl.when(i > 0)
    def _():
        for k in range(2):
            blocks_ref[(i - 1) * NW + j, k * Z : (k + 1) * Z] = f32_ref[2 + k].astype(jnp.bfloat16)

    @pl.when(i < NH - 1)
    def _():
        for k in range(2):
            blocks_ref[(i + 1) * NW + j, k * Z : (k + 1) * Z] = f32_ref[h + k].astype(jnp.bfloat16)


def turn_taps(fields, r, turned, last):
    parts = []
    for field in fields:
        for dc in range(3):
            piece = field if dc == 0 else pltpu.roll(field, LANES - dc, 1)
            parts.append(piece.astype(jnp.bfloat16))
    turned[r] = jnp.concatenate(parts[:8], axis=0).T
    last[r * Z : (r + 1) * Z] = parts[8]


def tap_rows(r, turned, last):
    rest = last[r * Z : (r + 3) * Z].T
    return jnp.concatenate([turned[r], turned[r + 1], turned[r + 2], rest], axis=1)


def entry_weights(wi_ref):
    order = [(dr, k) for dr in range(3) for k in range(8)] + [(dr, 8) for dr in range(3)]
    return jnp.concatenate([wi_ref[9 * (k // 3) + 3 * dr + k % 3] for dr, k in order], axis=0)


def entry_of(rows, wi, bias):
    got = jnp.dot(jnp.concatenate(rows, axis=0), wi, preferred_element_type=jnp.float32)
    return (got + bias).astype(jnp.bfloat16).astype(jnp.float32)


def active_of(entry, half_gain, ok):
    meansq = jnp.mean(entry * entry, axis=-1, keepdims=True)
    half = entry * jnp.where(ok, lax.rsqrt(meansq + 1e-06), 0.0) * half_gain
    return half + half * jnp.tanh(half)


def inside(size_ref):
    i, j = lax.axis_index("ha"), lax.axis_index("wa")
    h, w = size_ref[0:1, 0:1], size_ref[8:9, 0:1]
    pos = lax.broadcasted_iota(jnp.int32, (LANES, 1), 0)
    col = pos % SPAN
    col_ok = ((j > 0) | (col > 0)) & ((j < NW - 1) | (col <= w))

    def row_ok(r):
        return ((i > 0) | (r > 0)) & ((i < NH - 1) | (r <= h))

    return pos, col_ok, row_ok


def last_frames(own_ref, size_ref, wi_ref, bi_ref, gain_ref, act_ref, short_ref, turned, last):
    lane = lax.broadcasted_iota(jnp.int32, (Z, LANES), 1)
    for r in range(RE - 1):
        own = own_ref[r].astype(jnp.float32)
        nxt = own_ref[r + 1].astype(jnp.float32)
        fields = []
        for dt in range(3):
            a = own if dt == 0 else pltpu.roll(own, LANES - dt * SPAN, 1)
            b = nxt if dt == 2 else pltpu.roll(nxt, (2 - dt) * SPAN, 1)
            fields.append(jnp.where(lane < 2 * SPAN, a, b))
        turn_taps(fields, r, turned, last)
    wi = entry_weights(wi_ref)
    bias, half_gain = bi_ref[...].reshape(1, C), 0.5 * gain_ref[...].reshape(1, C)
    pos, col_ok, row_ok = inside(size_ref)
    steps = RA // 2
    for first, count in ((0, 4), (4, 3)):
        entry = entry_of([tap_rows(2 * q, turned, last) for q in range(first, first + count)], wi, bias)
        for q in range(first, first + count):
            e = entry[(q - first) * LANES : (q - first + 1) * LANES]
            r = 2 * q
            ok = col_ok & ((row_ok(r) & (pos < 2 * SPAN)) | (row_ok(r + 1) & (pos >= 2 * SPAN)))
            act_ref[q] = active_of(e, half_gain, ok)
            for k in range(2):
                short_ref[r + k] = jnp.concatenate(
                    [e[at + 1 : at + 1 + TW, :CO] for at in (2 * k * SPAN, (2 * k + 1) * SPAN)], axis=0
                )


def transform_weights(wm_ref, u_ref):
    for tap in range(9):
        ends = 0.5 * (wm_ref[tap].astype(jnp.float32) + wm_ref[18 + tap].astype(jnp.float32))
        mid = 0.5 * wm_ref[9 + tap].astype(jnp.float32)
        u_ref[0, tap] = (ends + mid).astype(jnp.bfloat16)
        u_ref[1, tap] = (ends - mid).astype(jnp.bfloat16)


def join_kernel(
    got_ref, own_ref, size_ref, wm_ref, ext_ref, u_ref, act_ref, short_ref, f32_ref,
):
    i, j = lax.axis_index("ha"), lax.axis_index("wa")
    h, w, hu = (jnp.max(size_ref[8 * k : 8 * k + 8].astype(jnp.float32)).astype(jnp.int32) for k in range(3))
    up, down = jnp.maximum(i - 1, 0), jnp.minimum(i + 1, NH - 1)
    lane = lanes_of()
    to_left, to_right = lane < 2, (lane >= w + 2) & (lane < w + 4)

    def strip(at, k, ok):
        return jnp.where(ok, got_ref[at, k * Z : (k + 1) * Z].astype(jnp.float32), 0.0)

    def sides(row):
        out = []
        for col, ok in ((jnp.maximum(j - 1, 0), j > 0), (jnp.minimum(j + 1, NW - 1), j < NW - 1)):
            row_ok = ok & (row >= 0) & (row < NH)
            out.append(strip(jnp.clip(row, 0, NH - 1) * NW + col, 0, row_ok))
        return out

    def put(at, base, pair, r):
        row = jnp.where(to_left, pltpu.roll(pair[0], (LANES - 2 * r) % LANES, 1), base)
        row = jnp.where(to_right, pltpu.roll(pair[1], (LANES + w + 2 - 2 * r) % LANES, 1), row)
        f32_ref[at] = row

    mid = sides(i)
    for r in range(TH):
        put(2 + r, own_ref[2 + r].astype(jnp.float32), mid, r)
    above, below = sides(i - 1), sides(i + 1)
    for k in range(2):
        put(k, strip(up * NW + j, k, i > 0), above, hu - 2 + k)
    for k in range(2):
        put(h + 2 + k, strip(down * NW + j, k, i < NH - 1), below, k)
    ext_ref[...] = f32_ref[...].astype(jnp.bfloat16)

    @pl.when(lax.axis_index("tm") % 2 == 1)
    def _():
        transform_weights(wm_ref, u_ref)


def ahead_kernel(
    wm_ref, wi_ref, bi_ref, gain_ref, own_ref, size_ref, u_in, act_in, short_in,
    u_ref, act_ref, short_ref, turned, last,
):
    @pl.when(lax.axis_index("tm") % 2 == 0)
    def _():
        transform_weights(wm_ref, u_ref)

    last_frames(own_ref, size_ref, wi_ref, bi_ref, gain_ref, act_ref, short_ref, turned, last)


def main_kernel(
    prev_ref, own_ref, size_ref, wi_ref, bi_ref, gain_ref, wm_ref, u_ref, act_ref, late_ref, bm_ref,
    out_ref, turned, last, lhs_ref, short_ref, acc_ref, made_ref, sems,
):
    lane = lax.broadcasted_iota(jnp.int32, (Z, LANES), 1)
    for r in range(RE):
        prev, own = prev_ref[r].astype(jnp.float32), own_ref[r].astype(jnp.float32)
        one = jnp.where(lane < 3 * SPAN, pltpu.roll(prev, 3 * SPAN, 1), pltpu.roll(own, 3 * SPAN, 1))
        two = jnp.where(lane < 2 * SPAN, pltpu.roll(prev, 2 * SPAN, 1), pltpu.roll(own, 2 * SPAN, 1))
        turn_taps((prev, one, two), r, turned, last)

    wi = entry_weights(wi_ref)
    bias, half_gain = bi_ref[...].reshape(1, C), 0.5 * gain_ref[...].reshape(1, C)
    w, h = size_ref[8:9, 0:1], size_ref[0:1, 0:1]
    pos, col_ok, row_ok = inside(size_ref)
    early = (lax.axis_index("tm") > 0) | (pos >= 2 * SPAN)

    def step(q):
        r = 2 * q
        entry = entry_of([tap_rows(r, turned, last), tap_rows(r + 1, turned, last)], wi, bias)
        yield
        ents = [entry[k * LANES : (k + 1) * LANES] for k in range(2)]
        acts = []
        for k in range(2):
            acts.append(active_of(ents[k], half_gain, col_ok & early & row_ok(r + k)))
            yield
        for k in range(2):
            frames = [acts[k][f * SPAN : (f + 1) * SPAN] for f in range(4)]
            frames += [act_ref[q, (2 * k + f) * SPAN : (2 * k + f + 1) * SPAN] for f in range(2)]
            m = (r + k) * PR
            for p in range(4):
                pair = []
                for a in (frames[:4], frames[2:]):
                    pair.append((a[0] - a[2], a[1] + a[2], a[2] - a[1], a[1] - a[3])[p])
                for dc in range(3):
                    lhs_ref[p, m : m + PR, dc * C : (dc + 1) * C] = jnp.concatenate(
                        [v[dc : dc + TW] for v in pair], axis=0
                    ).astype(jnp.bfloat16)
                if p % 2:
                    yield
            if 1 <= r + k <= TH:
                short_ref[r + k] = jnp.concatenate(
                    [ents[k][(2 + f) * SPAN + 1 : (2 + f) * SPAN + 1 + TW, :CO] for f in range(2)], axis=0
                )

    def plane(p):
        taps = (wm_ref[0:9], u_ref[0], u_ref[1], wm_ref[18:27])[p]
        return taps.reshape(9 * C, CO)

    def mid(p, first, rows):
        at = first * PR
        cuts = (0, 3456)
        for lo, hi in zip(cuts[:-1], cuts[1:]):
            parts = []
            for dr in range(3):
                a, b = max(lo - dr * 3 * C, 0), min(hi - dr * 3 * C, 3 * C)
                if a < b:
                    parts.append(lhs_ref[p, at + dr * PR : at + (dr + rows) * PR, a:b])
            got = jnp.dot(
                jnp.concatenate(parts, axis=1), plane(p)[lo:hi], preferred_element_type=jnp.float32
            )
            if lo == 0:
                acc_ref[p, at : at + rows * PR] = got
            else:
                acc_ref[p, at : at + rows * PR] += got
            yield

    def run(first, second, ratio):
        done = 0.0
        for _ in first:
            done += ratio
            while done >= 1.0:
                next(second, None)
                done -= 1.0
        for _ in second:
            pass

    def chain(parts):
        for part in parts:
            yield from part

    bias_m = bm_ref[...].reshape(1, CO)
    keep_col = lax.broadcasted_iota(jnp.int32, (TW, 1), 0) < w

    def write(half):
        for r in range(half * HALF, (half + 1) * HALF):
            ok = keep_col & (r < h)
            for pair in range(2):
                m = r * PR + pair * TW
                m0, m1, m2, m3 = (acc_ref[p, m : m + TW] for p in range(4))
                for f, mixed in ((2 * pair, m0 + m1 + m2), (2 * pair + 1, m1 - m2 - m3)):
                    short = (short_ref, late_ref)[pair][r + 1, (f % 2) * TW : (f % 2 + 1) * TW]
                    val = short + mixed + bias_m
                    made_ref[f, r] = jnp.where(ok, val, 0.0).astype(jnp.bfloat16)
            yield
        send(half).start()

    def send(half):
        part = pl.ds(half * HALF, HALF)
        return pltpu.make_async_copy(made_ref.at[:, part], out_ref.at[:, part], sems.at[half])

    for _ in chain(step(q) for q in range(4)):
        pass
    run(chain(mid(p, 0, HALF) for p in range(4)), chain(step(q) for q in range(4, 7)), 6.0)
    run(chain(mid(p, HALF, HALF) for p in range(4)), write(0), 2.0)
    for _ in write(1):
        pass
    send(0).wait()
    send(1).wait()


def per_device(
    latents, in_weight, in_bias, norm_gain, mid_weight, mid_bias, row_heights, col_widths
):
    flipped = jnp.transpose(latents, (0, 1, 3, 2))
    vmem = pl.BlockSpec(memory_space=VM)
    hbm = pl.BlockSpec(memory_space=HBM)

    def stay(*arrays):
        return [pltpu.with_memory_space_constraint(a, HBM) for a in arrays]

    bf16, f32 = jnp.bfloat16, jnp.float32
    limit = pltpu.CompilerParams(vmem_limit_bytes=4 * 1024 * 1024)
    blocks, own, sizes = pl.pallas_call(
        pack_kernel,
        out_shape=(
            VM((NH * NW, 2 * Z, LANES), bf16), VM((RE, Z, LANES), bf16), VM((24, LANES), jnp.int32)
        ),
        in_specs=[hbm] * 3,
        out_specs=(vmem,) * 3,
        scratch_shapes=[
            pltpu.VMEM((RE, Z, LANES), f32),
            pltpu.VMEM((F, TH, Z, TW), bf16),
            pltpu.SMEM((NH,), jnp.int32),
            pltpu.SMEM((NW,), jnp.int32),
            pltpu.SemaphoreType.DMA((3,)),
        ],
        compiler_params=limit,
        cost_estimate=pl.CostEstimate(flops=10_000_000_000, bytes_accessed=20_000_000, transcendentals=0),
    )(*stay(row_heights, col_widths, flipped))
    got = lax.all_to_all(blocks, ("ha", "wa"), 0, 0, tiled=True)
    ahead = (VM((2, 9, C, CO), bf16), VM((RA // 2, LANES, C), f32), VM((RA, PR, CO), f32))
    turned = [pltpu.VMEM((RE, LANES, LANES), bf16), pltpu.VMEM((RE * Z, LANES), bf16)]
    entry_params = (in_weight, in_bias, norm_gain)
    ext, *made = pl.pallas_call(
        join_kernel,
        out_shape=(VM((RE, Z, LANES), bf16), *ahead),
        in_specs=[vmem] * 4,
        out_specs=(vmem,) * 4,
        scratch_shapes=[pltpu.VMEM((RE, Z, LANES), f32)],
        compiler_params=limit,
    )(got, own, sizes, mid_weight)
    groups = lax.axis_size("tm")
    prev = lax.ppermute(ext, "tm", [(g, g + 1) for g in range(groups - 1)])
    made = pl.pallas_call(
        ahead_kernel,
        out_shape=ahead,
        in_specs=[vmem] * 9,
        out_specs=(vmem,) * 3,
        scratch_shapes=turned,
        input_output_aliases={6: 0, 7: 1, 8: 2},
        compiler_params=limit,
        cost_estimate=pl.CostEstimate(flops=400_000_000, bytes_accessed=8_000_000, transcendentals=400_000),
    )(mid_weight, *entry_params, ext, sizes, *made)
    return pl.pallas_call(
        main_kernel,
        out_shape=jax.ShapeDtypeStruct((F, TH, TW, CO), bf16),
        in_specs=[vmem] * 11,
        out_specs=hbm,
        scratch_shapes=[
            *turned,
            pltpu.VMEM((4, RA * PR, 3 * C), bf16),
            pltpu.VMEM((RA, PR, CO), f32),
            pltpu.VMEM((4, TH * PR, CO), f32),
            pltpu.VMEM((F, TH, TW, CO), bf16),
            pltpu.SemaphoreType.DMA((2,)),
        ],
        compiler_params=pltpu.CompilerParams(vmem_limit_bytes=32 * 1024 * 1024),
        cost_estimate=pl.CostEstimate(flops=4_500_000_000, bytes_accessed=8_000_000, transcendentals=1_000_000),
    )(prev, ext, sizes, *entry_params, mid_weight, *made, mid_bias)


def solution(mesh):
    placed = (P("tm", "ha", "wa", None), P(), P(), P(), P(), P(), P(), P())
    return jax.shard_map(
        per_device, mesh=mesh, in_specs=placed, out_specs=P("tm", "ha", "wa", None), check_vma=False
    )
```

```python
import jax
import jax.numpy as jnp
from jax import lax
from jax.experimental import pallas as pl
from jax.experimental.pallas import tpu as pltpu
from jax.sharding import PartitionSpec as P

F = 4
TH, TW = 12, 24
Z, C, CO = 16, 384, 256
NH, NW = 4, 4
LANES = 128
SPAN = 32
RE = TH + 4
RA = TH + 2
MR = F * TW
HALF = TH // 2
PR = 2 * TW

VM = pltpu.MemorySpace.VMEM
HBM = pltpu.MemorySpace.HBM


def lanes_of():
    return lax.broadcasted_iota(jnp.int32, (Z, LANES), 1) % SPAN


def name(pairs, sems):
    return [pltpu.make_async_copy(src, dst, sems.at[k]) for k, (src, dst) in enumerate(pairs)]


def fetch(pairs, sems):
    copies = name(pairs, sems)
    for copy in copies:
        copy.start()
    return copies


def pack_kernel(
    rh_hbm, cw_hbm, lat_hbm, blocks_ref, own_ref, size_ref, f32_ref, lat_ref, rh_ref, cw_ref, sems
):
    copies = fetch(((rh_hbm, rh_ref), (cw_hbm, cw_ref), (lat_hbm, lat_ref)), sems)
    i, j = lax.axis_index("ha"), lax.axis_index("wa")
    lane = lanes_of()
    blocks_ref[...] = jnp.zeros_like(blocks_ref)
    f32_ref[...] = jnp.zeros_like(f32_ref)
    for copy in copies:
        copy.wait()
    h, w = rh_ref[i], cw_ref[j]
    for k, size in enumerate((h, w, rh_ref[jnp.maximum(i - 1, 0)])):
        size_ref[8 * k : 8 * k + 8] = jnp.full((8, LANES), size, jnp.int32)
    for r in range(TH):
        for f in range(F):
            f32_ref[2 + r, :, f * SPAN + 2 : f * SPAN + 2 + TW] = lat_ref[f, r].astype(jnp.float32)
    right = jnp.zeros((Z, LANES), jnp.float32)
    left = jnp.zeros((Z, LANES), jnp.float32)
    for r in range(TH):
        row = f32_ref[2 + r]
        here = (lane // 2) == r
        right = jnp.where(here, pltpu.roll(row, (2 * r - w + LANES) % LANES, 1), right)
        left = jnp.where(here, pltpu.roll(row, (2 * r - 2) % LANES, 1), left)
    right = right.astype(jnp.bfloat16)
    left = left.astype(jnp.bfloat16)
    own_ref[...] = f32_ref[...].astype(jnp.bfloat16)
    for di in (-1, 0, 1):
        row_in = (i + di >= 0) & (i + di < NH)
        for dj, tile in ((-1, left), (1, right)):
            @pl.when(row_in & (j + dj >= 0) & (j + dj < NW))
            def _(di=di, dj=dj, tile=tile):
                blocks_ref[(i + di) * NW + j + dj, 0:Z] = tile

    @pl.when(i > 0)
    def _():
        for k in range(2):
            blocks_ref[(i - 1) * NW + j, k * Z : (k + 1) * Z] = f32_ref[2 + k].astype(jnp.bfloat16)

    @pl.when(i < NH - 1)
    def _():
        for k in range(2):
            blocks_ref[(i + 1) * NW + j, k * Z : (k + 1) * Z] = f32_ref[h + k].astype(jnp.bfloat16)


def turn_taps(fields, r, turned, last):
    parts = []
    for field in fields:
        for dc in range(3):
            piece = field if dc == 0 else pltpu.roll(field, LANES - dc, 1)
            parts.append(piece.astype(jnp.bfloat16))
    turned[r] = jnp.concatenate(parts[:8], axis=0).T
    last[r * Z : (r + 1) * Z] = parts[8]


def tap_rows(r, turned, last):
    rest = last[r * Z : (r + 3) * Z].T
    return jnp.concatenate([turned[r], turned[r + 1], turned[r + 2], rest], axis=1)


def entry_weights(wi_ref):
    order = [(dr, k) for dr in range(3) for k in range(8)] + [(dr, 8) for dr in range(3)]
    return jnp.concatenate([wi_ref[9 * (k // 3) + 3 * dr + k % 3] for dr, k in order], axis=0)


def entry_of(rows, wi, bias):
    got = jnp.dot(jnp.concatenate(rows, axis=0), wi, preferred_element_type=jnp.float32)
    return (got + bias).astype(jnp.bfloat16).astype(jnp.float32)


def active_of(entry, half_gain, ok):
    meansq = jnp.mean(entry * entry, axis=-1, keepdims=True)
    half = entry * jnp.where(ok, lax.rsqrt(meansq + 1e-06), 0.0) * half_gain
    return half + half * jnp.tanh(half)


def inside(size_ref):
    i, j = lax.axis_index("ha"), lax.axis_index("wa")
    h, w = size_ref[0:1, 0:1], size_ref[8:9, 0:1]
    pos = lax.broadcasted_iota(jnp.int32, (LANES, 1), 0)
    col = pos % SPAN
    col_ok = ((j > 0) | (col > 0)) & ((j < NW - 1) | (col <= w))

    def row_ok(r):
        return ((i > 0) | (r > 0)) & ((i < NH - 1) | (r <= h))

    return pos, col_ok, row_ok


PARTS = ((0, 4), (4, 3))


def last_frames(own_ref, size_ref, wi_ref, bi_ref, gain_ref, act_ref, short_ref, turned, last, parts):
    lane = lax.broadcasted_iota(jnp.int32, (Z, LANES), 1)
    for r in range(2 * parts[0][0], 2 * sum(parts[-1]) + 1):
        own = own_ref[r].astype(jnp.float32)
        nxt = own_ref[r + 1].astype(jnp.float32)
        fields = []
        for dt in range(3):
            a = own if dt == 0 else pltpu.roll(own, LANES - dt * SPAN, 1)
            b = nxt if dt == 2 else pltpu.roll(nxt, (2 - dt) * SPAN, 1)
            fields.append(jnp.where(lane < 2 * SPAN, a, b))
        turn_taps(fields, r, turned, last)
    wi = entry_weights(wi_ref)
    bias, half_gain = bi_ref[...].reshape(1, C), 0.5 * gain_ref[...].reshape(1, C)
    pos, col_ok, row_ok = inside(size_ref)
    for first, count in parts:
        entry = entry_of([tap_rows(2 * q, turned, last) for q in range(first, first + count)], wi, bias)
        for q in range(first, first + count):
            e = entry[(q - first) * LANES : (q - first + 1) * LANES]
            r = 2 * q
            ok = col_ok & ((row_ok(r) & (pos < 2 * SPAN)) | (row_ok(r + 1) & (pos >= 2 * SPAN)))
            act_ref[q] = active_of(e, half_gain, ok)
            for k in range(2):
                short_ref[r + k] = jnp.concatenate(
                    [e[at + 1 : at + 1 + TW, :CO] for at in (2 * k * SPAN, (2 * k + 1) * SPAN)], axis=0
                )


def transform_weights(wm_ref, u_ref):
    for tap in range(9):
        ends = wm_ref[tap].astype(jnp.float32) + wm_ref[18 + tap].astype(jnp.float32)
        mid = wm_ref[9 + tap].astype(jnp.float32)
        u_ref[0, tap] = (ends + mid).astype(jnp.bfloat16)
        u_ref[1, tap] = (ends - mid).astype(jnp.bfloat16)


def join_kernel(
    got_ref, own_ref, size_ref, wm_ref, wi_ref, bi_ref, gain_ref,
    ext_ref, u_ref, act_ref, short_ref, f32_ref, turned, last,
):
    i, j = lax.axis_index("ha"), lax.axis_index("wa")
    h, w, hu = (jnp.max(size_ref[8 * k : 8 * k + 8].astype(jnp.float32)).astype(jnp.int32) for k in range(3))
    up, down = jnp.maximum(i - 1, 0), jnp.minimum(i + 1, NH - 1)
    lane = lanes_of()
    to_left, to_right = lane < 2, (lane >= w + 2) & (lane < w + 4)

    def strip(at, k, ok):
        return jnp.where(ok, got_ref[at, k * Z : (k + 1) * Z].astype(jnp.float32), 0.0)

    def sides(row):
        out = []
        for col, ok in ((jnp.maximum(j - 1, 0), j > 0), (jnp.minimum(j + 1, NW - 1), j < NW - 1)):
            row_ok = ok & (row >= 0) & (row < NH)
            out.append(strip(jnp.clip(row, 0, NH - 1) * NW + col, 0, row_ok))
        return out

    def put(at, base, pair, r):
        row = jnp.where(to_left, pltpu.roll(pair[0], (LANES - 2 * r) % LANES, 1), base)
        row = jnp.where(to_right, pltpu.roll(pair[1], (LANES + w + 2 - 2 * r) % LANES, 1), row)
        f32_ref[at] = row

    mid = sides(i)
    for r in range(TH):
        put(2 + r, own_ref[2 + r].astype(jnp.float32), mid, r)
    above, below = sides(i - 1), sides(i + 1)
    for k in range(2):
        put(k, strip(up * NW + j, k, i > 0), above, hu - 2 + k)
    for k in range(2):
        put(h + 2 + k, strip(down * NW + j, k, i < NH - 1), below, k)
    ext_ref[...] = f32_ref[...].astype(jnp.bfloat16)

    @pl.when(lax.axis_index("tm") % 2 == 1)
    def _():
        transform_weights(wm_ref, u_ref)
        last_frames(
            ext_ref, size_ref, wi_ref, bi_ref, gain_ref, act_ref, short_ref, turned, last, PARTS[:1]
        )


def ahead_kernel(
    wm_ref, wi_ref, bi_ref, gain_ref, own_ref, size_ref, u_in, act_in, short_in,
    u_ref, act_ref, short_ref, turned, last,
):
    @pl.when(lax.axis_index("tm") % 2 == 0)
    def _():
        transform_weights(wm_ref, u_ref)
        last_frames(
            own_ref, size_ref, wi_ref, bi_ref, gain_ref, act_ref, short_ref, turned, last, PARTS
        )

    @pl.when(lax.axis_index("tm") % 2 == 1)
    def _():
        last_frames(
            own_ref, size_ref, wi_ref, bi_ref, gain_ref, act_ref, short_ref, turned, last, PARTS[1:]
        )


def main_kernel(
    prev_ref, own_ref, size_ref, wi_ref, bi_ref, gain_ref, wm_ref, u_ref, act_ref, late_ref, bm_ref,
    out_ref, turned, last, lhs_ref, short_ref, acc_ref, made_ref, sems,
):
    lane = lax.broadcasted_iota(jnp.int32, (Z, LANES), 1)
    for r in range(RE):
        prev, own = prev_ref[r].astype(jnp.float32), own_ref[r].astype(jnp.float32)
        one = jnp.where(lane < 3 * SPAN, pltpu.roll(prev, 3 * SPAN, 1), pltpu.roll(own, 3 * SPAN, 1))
        two = jnp.where(lane < 2 * SPAN, pltpu.roll(prev, 2 * SPAN, 1), pltpu.roll(own, 2 * SPAN, 1))
        turn_taps((prev, one, two), r, turned, last)

    wi = entry_weights(wi_ref)
    bias, half_gain = bi_ref[...].reshape(1, C), 0.5 * gain_ref[...].reshape(1, C)
    w, h = size_ref[8:9, 0:1], size_ref[0:1, 0:1]
    pos, col_ok, row_ok = inside(size_ref)
    early = (lax.axis_index("tm") > 0) | (pos >= 2 * SPAN)

    def step(q):
        r = 2 * q
        entry = entry_of([tap_rows(r, turned, last), tap_rows(r + 1, turned, last)], wi, bias)
        yield
        ents = [entry[k * LANES : (k + 1) * LANES] for k in range(2)]
        acts = []
        for k in range(2):
            acts.append(active_of(ents[k], half_gain, col_ok & early & row_ok(r + k)))
            yield
        for k in range(2):
            frames = [acts[k][f * SPAN : (f + 1) * SPAN] for f in range(4)]
            frames += [act_ref[q, (2 * k + f) * SPAN : (2 * k + f + 1) * SPAN] for f in range(2)]
            m = (r + k) * PR
            for p in range(4):
                pair = []
                for a in (frames[:4], frames[2:]):
                    pair.append((a[0] - a[2], a[1] + a[2], a[2] - a[1], a[1] - a[3])[p])
                for dc in range(3):
                    lhs_ref[p, m : m + PR, dc * C : (dc + 1) * C] = jnp.concatenate(
                        [v[dc : dc + TW] for v in pair], axis=0
                    ).astype(jnp.bfloat16)
                if p % 2:
                    yield
            if 1 <= r + k <= TH:
                short_ref[r + k] = jnp.concatenate(
                    [ents[k][(2 + f) * SPAN + 1 : (2 + f) * SPAN + 1 + TW, :CO] for f in range(2)], axis=0
                )

    def plane(p):
        taps = (wm_ref[0:9], u_ref[0], u_ref[1], wm_ref[18:27])[p]
        return taps.reshape(9 * C, CO)

    def mid(p, first, rows):
        at = first * PR
        cuts = (0, 3456)
        for lo, hi in zip(cuts[:-1], cuts[1:]):
            parts = []
            for dr in range(3):
                a, b = max(lo - dr * 3 * C, 0), min(hi - dr * 3 * C, 3 * C)
                if a < b:
                    parts.append(lhs_ref[p, at + dr * PR : at + (dr + rows) * PR, a:b])
            got = jnp.dot(
                jnp.concatenate(parts, axis=1), plane(p)[lo:hi], preferred_element_type=jnp.float32
            )
            if lo == 0:
                acc_ref[p, at : at + rows * PR] = got
            else:
                acc_ref[p, at : at + rows * PR] += got
            yield

    def run(first, second, ratio):
        done = 0.0
        for _ in first:
            done += ratio
            while done >= 1.0:
                next(second, None)
                done -= 1.0
        for _ in second:
            pass

    def chain(parts):
        for part in parts:
            yield from part

    bias_m = bm_ref[...].reshape(1, CO)
    keep_col = lax.broadcasted_iota(jnp.int32, (TW, 1), 0) < w

    def write(half):
        for r in range(half * HALF, (half + 1) * HALF):
            ok = keep_col & (r < h)
            for pair in range(2):
                m = r * PR + pair * TW
                m0, m1, m2, m3 = (acc_ref[p, m : m + TW] for p in range(4))
                for f, mixed in ((2 * pair, m0 + 0.5 * (m1 + m2)), (2 * pair + 1, 0.5 * (m1 - m2) - m3)):
                    short = (short_ref, late_ref)[pair][r + 1, (f % 2) * TW : (f % 2 + 1) * TW]
                    val = short + mixed + bias_m
                    made_ref[f, r] = jnp.where(ok, val, 0.0).astype(jnp.bfloat16)
            yield
        send(half).start()

    def send(half):
        part = pl.ds(half * HALF, HALF)
        return pltpu.make_async_copy(made_ref.at[:, part], out_ref.at[:, part], sems.at[half])

    for _ in chain(step(q) for q in range(4)):
        pass
    run(chain(mid(p, 0, HALF) for p in range(4)), chain(step(q) for q in range(4, 7)), 6.0)
    run(chain(mid(p, HALF, HALF) for p in range(4)), write(0), 2.0)
    for _ in write(1):
        pass
    send(0).wait()
    send(1).wait()


def per_device(
    latents, in_weight, in_bias, norm_gain, mid_weight, mid_bias, row_heights, col_widths
):
    flipped = jnp.transpose(latents, (0, 1, 3, 2))
    vmem = pl.BlockSpec(memory_space=VM)
    hbm = pl.BlockSpec(memory_space=HBM)

    def stay(*arrays):
        return [pltpu.with_memory_space_constraint(a, HBM) for a in arrays]

    bf16, f32 = jnp.bfloat16, jnp.float32
    limit = pltpu.CompilerParams(vmem_limit_bytes=4 * 1024 * 1024)
    blocks, own, sizes = pl.pallas_call(
        pack_kernel,
        out_shape=(
            VM((NH * NW, 2 * Z, LANES), bf16), VM((RE, Z, LANES), bf16), VM((24, LANES), jnp.int32)
        ),
        in_specs=[hbm] * 3,
        out_specs=(vmem,) * 3,
        scratch_shapes=[
            pltpu.VMEM((RE, Z, LANES), f32),
            pltpu.VMEM((F, TH, Z, TW), bf16),
            pltpu.SMEM((NH,), jnp.int32),
            pltpu.SMEM((NW,), jnp.int32),
            pltpu.SemaphoreType.DMA((3,)),
        ],
        compiler_params=limit,
        cost_estimate=pl.CostEstimate(flops=10_000_000_000, bytes_accessed=20_000_000, transcendentals=0),
    )(*stay(row_heights, col_widths, flipped))
    got = lax.all_to_all(blocks, ("ha", "wa"), 0, 0, tiled=True)
    ahead = (VM((2, 9, C, CO), bf16), VM((RA // 2, LANES, C), f32), VM((RA, PR, CO), f32))
    turned = [pltpu.VMEM((RE, LANES, LANES), bf16), pltpu.VMEM((RE * Z, LANES), bf16)]
    entry_params = (in_weight, in_bias, norm_gain)
    ext, *made = pl.pallas_call(
        join_kernel,
        out_shape=(VM((RE, Z, LANES), bf16), *ahead),
        in_specs=[vmem] * 7,
        out_specs=(vmem,) * 4,
        scratch_shapes=[pltpu.VMEM((RE, Z, LANES), f32), *turned],
        compiler_params=limit,
    )(got, own, sizes, mid_weight, *entry_params)
    groups = lax.axis_size("tm")
    prev = lax.ppermute(ext, "tm", [(g, g + 1) for g in range(groups - 1)])
    made = pl.pallas_call(
        ahead_kernel,
        out_shape=ahead,
        in_specs=[vmem] * 9,
        out_specs=(vmem,) * 3,
        scratch_shapes=turned,
        input_output_aliases={6: 0, 7: 1, 8: 2},
        compiler_params=limit,
        cost_estimate=pl.CostEstimate(flops=400_000_000, bytes_accessed=8_000_000, transcendentals=400_000),
    )(mid_weight, *entry_params, ext, sizes, *made)
    return pl.pallas_call(
        main_kernel,
        out_shape=jax.ShapeDtypeStruct((F, TH, TW, CO), bf16),
        in_specs=[vmem] * 11,
        out_specs=hbm,
        scratch_shapes=[
            *turned,
            pltpu.VMEM((4, RA * PR, 3 * C), bf16),
            pltpu.VMEM((RA, PR, CO), f32),
            pltpu.VMEM((4, TH * PR, CO), f32),
            pltpu.VMEM((F, TH, TW, CO), bf16),
            pltpu.SemaphoreType.DMA((2,)),
        ],
        compiler_params=pltpu.CompilerParams(vmem_limit_bytes=32 * 1024 * 1024),
        cost_estimate=pl.CostEstimate(flops=4_500_000_000, bytes_accessed=8_000_000, transcendentals=1_000_000),
    )(prev, ext, sizes, *entry_params, mid_weight, *made, mid_bias)


def solution(mesh):
    placed = (P("tm", "ha", "wa", None), P(), P(), P(), P(), P(), P(), P())
    return jax.shard_map(
        per_device, mesh=mesh, in_specs=placed, out_specs=P("tm", "ha", "wa", None), check_vma=False
    )
```

```python
import jax
import jax.numpy as jnp
from jax import lax
from jax.experimental import pallas as pl
from jax.experimental.pallas import tpu as pltpu
from jax.sharding import PartitionSpec as P

F = 4
TH, TW = 12, 24
Z, C, CO = 16, 384, 256
NH, NW = 4, 4
LANES = 128
SPAN = 32
RE = TH + 4
RA = TH + 2
MR = F * TW
HALF = TH // 2
PR = 2 * TW

VM = pltpu.MemorySpace.VMEM
HBM = pltpu.MemorySpace.HBM


def lanes_of():
    return lax.broadcasted_iota(jnp.int32, (Z, LANES), 1) % SPAN


def name(pairs, sems):
    return [pltpu.make_async_copy(src, dst, sems.at[k]) for k, (src, dst) in enumerate(pairs)]


def fetch(pairs, sems):
    copies = name(pairs, sems)
    for copy in copies:
        copy.start()
    return copies


def pack_kernel(
    rh_hbm, cw_hbm, lat_hbm, blocks_ref, own_ref, size_ref, f32_ref, lat_ref, rh_ref, cw_ref, sems
):
    copies = fetch(((rh_hbm, rh_ref), (cw_hbm, cw_ref), (lat_hbm, lat_ref)), sems)
    i, j = lax.axis_index("ha"), lax.axis_index("wa")
    lane = lanes_of()
    blocks_ref[...] = jnp.zeros_like(blocks_ref)
    f32_ref[...] = jnp.zeros_like(f32_ref)
    for copy in copies:
        copy.wait()
    h, w = rh_ref[i], cw_ref[j]
    for k, size in enumerate((h, w, rh_ref[jnp.maximum(i - 1, 0)])):
        size_ref[8 * k : 8 * k + 8] = jnp.full((8, LANES), size, jnp.int32)
    for r in range(TH):
        for f in range(F):
            f32_ref[2 + r, :, f * SPAN + 2 : f * SPAN + 2 + TW] = lat_ref[f, r].astype(jnp.float32)
    right = jnp.zeros((Z, LANES), jnp.float32)
    left = jnp.zeros((Z, LANES), jnp.float32)
    for r in range(TH):
        row = f32_ref[2 + r]
        here = (lane // 2) == r
        right = jnp.where(here, pltpu.roll(row, (2 * r - w + LANES) % LANES, 1), right)
        left = jnp.where(here, pltpu.roll(row, (2 * r - 2) % LANES, 1), left)
    right = right.astype(jnp.bfloat16)
    left = left.astype(jnp.bfloat16)
    own_ref[...] = f32_ref[...].astype(jnp.bfloat16)
    for di in (-1, 0, 1):
        row_in = (i + di >= 0) & (i + di < NH)
        for dj, tile in ((-1, left), (1, right)):
            @pl.when(row_in & (j + dj >= 0) & (j + dj < NW))
            def _(di=di, dj=dj, tile=tile):
                blocks_ref[(i + di) * NW + j + dj, 0:Z] = tile

    @pl.when(i > 0)
    def _():
        for k in range(2):
            blocks_ref[(i - 1) * NW + j, k * Z : (k + 1) * Z] = f32_ref[2 + k].astype(jnp.bfloat16)

    @pl.when(i < NH - 1)
    def _():
        for k in range(2):
            blocks_ref[(i + 1) * NW + j, k * Z : (k + 1) * Z] = f32_ref[h + k].astype(jnp.bfloat16)


def turn_taps(fields, r, turned, last):
    parts = []
    for field in fields:
        for dc in range(3):
            piece = field if dc == 0 else pltpu.roll(field, LANES - dc, 1)
            parts.append(piece.astype(jnp.bfloat16))
    turned[r] = jnp.concatenate(parts[:8], axis=0).T
    last[r * Z : (r + 1) * Z] = parts[8]


def tap_rows(r, turned, last):
    rest = last[r * Z : (r + 3) * Z].T
    return jnp.concatenate([turned[r], turned[r + 1], turned[r + 2], rest], axis=1)


def entry_weights(wi_ref):
    order = [(dr, k) for dr in range(3) for k in range(8)] + [(dr, 8) for dr in range(3)]
    return jnp.concatenate([wi_ref[9 * (k // 3) + 3 * dr + k % 3] for dr, k in order], axis=0)


def entry_of(rows, wi, bias):
    got = jnp.dot(jnp.concatenate(rows, axis=0), wi, preferred_element_type=jnp.float32)
    return (got + bias).astype(jnp.bfloat16).astype(jnp.float32)


def active_of(entry, half_gain, ok):
    meansq = jnp.mean(entry * entry, axis=-1, keepdims=True)
    half = entry * jnp.where(ok, lax.rsqrt(meansq + 1e-06), 0.0) * half_gain
    return half + half * jnp.tanh(half)


def inside(size_ref):
    i, j = lax.axis_index("ha"), lax.axis_index("wa")
    h, w = size_ref[0:1, 0:1], size_ref[8:9, 0:1]
    pos = lax.broadcasted_iota(jnp.int32, (LANES, 1), 0)
    col = pos % SPAN
    col_ok = ((j > 0) | (col > 0)) & ((j < NW - 1) | (col <= w))

    def row_ok(r):
        return ((i > 0) | (r > 0)) & ((i < NH - 1) | (r <= h))

    return pos, col_ok, row_ok


PARTS = ((0, 4), (4, 3))


def last_frames(own_ref, size_ref, wi_ref, bi_ref, gain_ref, act_ref, short_ref, turned, last, parts):
    lane = lax.broadcasted_iota(jnp.int32, (Z, LANES), 1)
    for r in range(2 * parts[0][0], 2 * sum(parts[-1]) + 1):
        own = own_ref[r].astype(jnp.float32)
        nxt = own_ref[r + 1].astype(jnp.float32)
        fields = []
        for dt in range(3):
            a = own if dt == 0 else pltpu.roll(own, LANES - dt * SPAN, 1)
            b = nxt if dt == 2 else pltpu.roll(nxt, (2 - dt) * SPAN, 1)
            fields.append(jnp.where(lane < 2 * SPAN, a, b))
        turn_taps(fields, r, turned, last)
    wi = entry_weights(wi_ref)
    bias, half_gain = bi_ref[...].reshape(1, C), 0.5 * gain_ref[...].reshape(1, C)
    pos, col_ok, row_ok = inside(size_ref)
    for first, count in parts:
        entry = entry_of([tap_rows(2 * q, turned, last) for q in range(first, first + count)], wi, bias)
        for q in range(first, first + count):
            e = entry[(q - first) * LANES : (q - first + 1) * LANES]
            r = 2 * q
            ok = col_ok & ((row_ok(r) & (pos < 2 * SPAN)) | (row_ok(r + 1) & (pos >= 2 * SPAN)))
            act_ref[q] = active_of(e, half_gain, ok)
            for k in range(2):
                short_ref[r + k] = jnp.concatenate(
                    [e[at + 1 : at + 1 + TW, :CO] for at in (2 * k * SPAN, (2 * k + 1) * SPAN)], axis=0
                )


def transform_weights(wm_ref, u_ref):
    for tap in range(9):
        ends = wm_ref[tap].astype(jnp.float32) + wm_ref[18 + tap].astype(jnp.float32)
        mid = wm_ref[9 + tap].astype(jnp.float32)
        u_ref[0, tap] = (ends + mid).astype(jnp.bfloat16)
        u_ref[1, tap] = (ends - mid).astype(jnp.bfloat16)


def join_kernel(
    got_ref, own_ref, size_ref, wm_ref, wi_ref, bi_ref, gain_ref,
    ext_ref, u_ref, act_ref, short_ref, f32_ref, turned, last,
):
    i, j = lax.axis_index("ha"), lax.axis_index("wa")
    h, w, hu = (jnp.max(size_ref[8 * k : 8 * k + 8].astype(jnp.float32)).astype(jnp.int32) for k in range(3))
    up, down = jnp.maximum(i - 1, 0), jnp.minimum(i + 1, NH - 1)
    lane = lanes_of()
    to_left, to_right = lane < 2, (lane >= w + 2) & (lane < w + 4)

    def strip(at, k, ok):
        return jnp.where(ok, got_ref[at, k * Z : (k + 1) * Z].astype(jnp.float32), 0.0)

    def sides(row):
        out = []
        for col, ok in ((jnp.maximum(j - 1, 0), j > 0), (jnp.minimum(j + 1, NW - 1), j < NW - 1)):
            row_ok = ok & (row >= 0) & (row < NH)
            out.append(strip(jnp.clip(row, 0, NH - 1) * NW + col, 0, row_ok))
        return out

    def put(at, base, pair, r):
        row = jnp.where(to_left, pltpu.roll(pair[0], (LANES - 2 * r) % LANES, 1), base)
        row = jnp.where(to_right, pltpu.roll(pair[1], (LANES + w + 2 - 2 * r) % LANES, 1), row)
        f32_ref[at] = row

    mid = sides(i)
    for r in range(TH):
        put(2 + r, own_ref[2 + r].astype(jnp.float32), mid, r)
    above, below = sides(i - 1), sides(i + 1)
    for k in range(2):
        put(k, strip(up * NW + j, k, i > 0), above, hu - 2 + k)
    for k in range(2):
        put(h + 2 + k, strip(down * NW + j, k, i < NH - 1), below, k)
    ext_ref[...] = f32_ref[...].astype(jnp.bfloat16)

    @pl.when(lax.axis_index("tm") % 2 == 1)
    def _():
        transform_weights(wm_ref, u_ref)
        last_frames(
            ext_ref, size_ref, wi_ref, bi_ref, gain_ref, act_ref, short_ref, turned, last, PARTS[:1]
        )


def ahead_kernel(
    wm_ref, wi_ref, bi_ref, gain_ref, own_ref, size_ref, u_in, act_in, short_in,
    u_ref, act_ref, short_ref, turned, last,
):
    @pl.when(lax.axis_index("tm") % 2 == 0)
    def _():
        transform_weights(wm_ref, u_ref)
        last_frames(
            own_ref, size_ref, wi_ref, bi_ref, gain_ref, act_ref, short_ref, turned, last, PARTS
        )

    @pl.when(lax.axis_index("tm") % 2 == 1)
    def _():
        last_frames(
            own_ref, size_ref, wi_ref, bi_ref, gain_ref, act_ref, short_ref, turned, last, PARTS[1:]
        )


def main_kernel(
    prev_ref, own_ref, size_ref, wi_ref, bi_ref, gain_ref, wm_ref, u_ref, act_ref, late_ref, bm_ref,
    out_ref, turned, last, lhs_ref, short_ref, acc_ref, made_ref, sems,
):
    lane = lax.broadcasted_iota(jnp.int32, (Z, LANES), 1)
    for r in range(RE):
        prev, own = prev_ref[r].astype(jnp.float32), own_ref[r].astype(jnp.float32)
        one = jnp.where(lane < 3 * SPAN, pltpu.roll(prev, 3 * SPAN, 1), pltpu.roll(own, 3 * SPAN, 1))
        two = jnp.where(lane < 2 * SPAN, pltpu.roll(prev, 2 * SPAN, 1), pltpu.roll(own, 2 * SPAN, 1))
        turn_taps((prev, one, two), r, turned, last)

    wi = entry_weights(wi_ref)
    bias, half_gain = bi_ref[...].reshape(1, C), 0.5 * gain_ref[...].reshape(1, C)
    w, h = size_ref[8:9, 0:1], size_ref[0:1, 0:1]
    pos, col_ok, row_ok = inside(size_ref)
    early = (lax.axis_index("tm") > 0) | (pos >= 2 * SPAN)

    def step(q):
        r = 2 * q
        entry = entry_of([tap_rows(r, turned, last), tap_rows(r + 1, turned, last)], wi, bias)
        yield
        ents = [entry[k * LANES : (k + 1) * LANES] for k in range(2)]
        acts = []
        for k in range(2):
            acts.append(active_of(ents[k], half_gain, col_ok & early & row_ok(r + k)))
            yield
        for k in range(2):
            frames = [acts[k][f * SPAN : (f + 1) * SPAN] for f in range(4)]
            frames += [act_ref[q, (2 * k + f) * SPAN : (2 * k + f + 1) * SPAN] for f in range(2)]
            m = (r + k) * PR
            for p in range(4):
                pair = []
                for a in (frames[:4], frames[2:]):
                    pair.append((a[0] - a[2], a[1] + a[2], a[2] - a[1], a[1] - a[3])[p])
                for dc in range(3):
                    lhs_ref[p, m : m + PR, dc * C : (dc + 1) * C] = jnp.concatenate(
                        [v[dc : dc + TW] for v in pair], axis=0
                    ).astype(jnp.bfloat16)
                if p % 2:
                    yield
            if 1 <= r + k <= TH:
                short_ref[r + k] = jnp.concatenate(
                    [ents[k][(2 + f) * SPAN + 1 : (2 + f) * SPAN + 1 + TW, :CO] for f in range(2)], axis=0
                )

    def plane(p):
        taps = (wm_ref[0:9], u_ref[0], u_ref[1], wm_ref[18:27])[p]
        return taps.reshape(9 * C, CO)

    def mid(p, first, rows):
        at = first * PR
        cuts = (0, 3456)
        for lo, hi in zip(cuts[:-1], cuts[1:]):
            parts = []
            for dr in range(3):
                a, b = max(lo - dr * 3 * C, 0), min(hi - dr * 3 * C, 3 * C)
                if a < b:
                    parts.append(lhs_ref[p, at + dr * PR : at + (dr + rows) * PR, a:b])
            got = jnp.dot(
                jnp.concatenate(parts, axis=1), plane(p)[lo:hi], preferred_element_type=jnp.float32
            )
            if lo == 0:
                acc_ref[p, at : at + rows * PR] = got
            else:
                acc_ref[p, at : at + rows * PR] += got
            yield

    def run(first, second, ratio):
        done = 0.0
        for _ in first:
            done += ratio
            while done >= 1.0:
                next(second, None)
                done -= 1.0
        for _ in second:
            pass

    def chain(parts):
        for part in parts:
            yield from part

    bias_m = bm_ref[...].reshape(1, CO)
    keep_col = lax.broadcasted_iota(jnp.int32, (TW, 1), 0) < w

    def write(half):
        for r in range(half * HALF, (half + 1) * HALF):
            ok = keep_col & (r < h)
            for pair in range(2):
                m = r * PR + pair * TW
                m0, m1, m2, m3 = (acc_ref[p, m : m + TW] for p in range(4))
                for f, mixed in ((2 * pair, m0 + 0.5 * (m1 + m2)), (2 * pair + 1, 0.5 * (m1 - m2) - m3)):
                    short = (short_ref, late_ref)[pair][r + 1, (f % 2) * TW : (f % 2 + 1) * TW]
                    val = short + mixed + bias_m
                    made_ref[f, r] = jnp.where(ok, val, 0.0).astype(jnp.bfloat16)
            yield
        send(half).start()

    def send(half):
        part = pl.ds(half * HALF, HALF)
        return pltpu.make_async_copy(made_ref.at[:, part], out_ref.at[:, part], sems.at[half])

    for _ in chain(step(q) for q in range(4)):
        pass
    run(chain(mid(p, 0, HALF) for p in range(4)), chain(step(q) for q in range(4, 7)), 4.0)
    run(chain(mid(p, HALF, HALF) for p in range(4)), write(0), 2.0)
    for _ in write(1):
        pass
    send(0).wait()
    send(1).wait()


def per_device(
    latents, in_weight, in_bias, norm_gain, mid_weight, mid_bias, row_heights, col_widths
):
    flipped = jnp.transpose(latents, (0, 1, 3, 2))
    vmem = pl.BlockSpec(memory_space=VM)
    hbm = pl.BlockSpec(memory_space=HBM)

    def stay(*arrays):
        return [pltpu.with_memory_space_constraint(a, HBM) for a in arrays]

    bf16, f32 = jnp.bfloat16, jnp.float32
    limit = pltpu.CompilerParams(vmem_limit_bytes=4 * 1024 * 1024)
    blocks, own, sizes = pl.pallas_call(
        pack_kernel,
        out_shape=(
            VM((NH * NW, 2 * Z, LANES), bf16), VM((RE, Z, LANES), bf16), VM((24, LANES), jnp.int32)
        ),
        in_specs=[hbm] * 3,
        out_specs=(vmem,) * 3,
        scratch_shapes=[
            pltpu.VMEM((RE, Z, LANES), f32),
            pltpu.VMEM((F, TH, Z, TW), bf16),
            pltpu.SMEM((NH,), jnp.int32),
            pltpu.SMEM((NW,), jnp.int32),
            pltpu.SemaphoreType.DMA((3,)),
        ],
        compiler_params=limit,
        cost_estimate=pl.CostEstimate(flops=10_000_000_000, bytes_accessed=20_000_000, transcendentals=0),
    )(*stay(row_heights, col_widths, flipped))
    got = lax.all_to_all(blocks, ("ha", "wa"), 0, 0, tiled=True)
    ahead = (VM((2, 9, C, CO), bf16), VM((RA // 2, LANES, C), f32), VM((RA, PR, CO), f32))
    turned = [pltpu.VMEM((RE, LANES, LANES), bf16), pltpu.VMEM((RE * Z, LANES), bf16)]
    entry_params = (in_weight, in_bias, norm_gain)
    ext, *made = pl.pallas_call(
        join_kernel,
        out_shape=(VM((RE, Z, LANES), bf16), *ahead),
        in_specs=[vmem] * 7,
        out_specs=(vmem,) * 4,
        scratch_shapes=[pltpu.VMEM((RE, Z, LANES), f32), *turned],
        compiler_params=limit,
    )(got, own, sizes, mid_weight, *entry_params)
    groups = lax.axis_size("tm")
    prev = lax.ppermute(ext, "tm", [(g, g + 1) for g in range(groups - 1)])
    made = pl.pallas_call(
        ahead_kernel,
        out_shape=ahead,
        in_specs=[vmem] * 9,
        out_specs=(vmem,) * 3,
        scratch_shapes=turned,
        input_output_aliases={6: 0, 7: 1, 8: 2},
        compiler_params=limit,
        cost_estimate=pl.CostEstimate(flops=400_000_000, bytes_accessed=8_000_000, transcendentals=400_000),
    )(mid_weight, *entry_params, ext, sizes, *made)
    return pl.pallas_call(
        main_kernel,
        out_shape=jax.ShapeDtypeStruct((F, TH, TW, CO), bf16),
        in_specs=[vmem] * 11,
        out_specs=hbm,
        scratch_shapes=[
            *turned,
            pltpu.VMEM((4, RA * PR, 3 * C), bf16),
            pltpu.VMEM((RA, PR, CO), f32),
            pltpu.VMEM((4, TH * PR, CO), f32),
            pltpu.VMEM((F, TH, TW, CO), bf16),
            pltpu.SemaphoreType.DMA((2,)),
        ],
        compiler_params=pltpu.CompilerParams(vmem_limit_bytes=32 * 1024 * 1024),
        cost_estimate=pl.CostEstimate(flops=4_500_000_000, bytes_accessed=8_000_000, transcendentals=1_000_000),
    )(prev, ext, sizes, *entry_params, mid_weight, *made, mid_bias)


def solution(mesh):
    placed = (P("tm", "ha", "wa", None), P(), P(), P(), P(), P(), P(), P())
    return jax.shard_map(
        per_device, mesh=mesh, in_specs=placed, out_specs=P("tm", "ha", "wa", None), check_vma=False
    )
```
